32 devices in a mesh: groups: 2 (over y), choice: 4 (over z), fsdp: 4 (over x, core).
Axes of the slice: x: 2, y: 2, z: 4, core: 2. Of those that a mesh axis runs over, the one named last changes fastest.
Arguments:
- hidden: bfloat16 [2048, 4096], P(('groups', 'choice'), 'fsdp'), parts along dimension 0, may hold values from -6 to 6
- norm_gain: float32 [4096], replicated, may hold values from 0.25 to 1.75
- query_weight: bfloat16 [4096, 4096], P('choice', 'fsdp'), may hold values from -0.09375 to 0.09375
- out_weight: bfloat16 [4096, 4096], P('fsdp', 'choice'), may hold values from -0.09375 to 0.09375
- enc_keys: bfloat16 [8, 256, 4096], P(('groups', 'choice'), None, 'fsdp'), parts along dimension 0, may hold values from -480 to 480
- enc_values: bfloat16 [8, 256, 4096], P(('groups', 'choice'), None, 'fsdp'), parts along dimension 0, may hold values from -24 to 24
- slot_question: int32 [32], P(('groups', 'choice')), parts along dimension 0, may hold values from 0 to 3, as said below
- answer_len: int32 [32], P(('groups', 'choice')), parts along dimension 0, may hold values from 16 to 64
Outputs:
- output: bfloat16 [2048, 4096], P(('groups', 'choice', 'fsdp')), parts along dimension 0
The draws below stay inside these ranges and needn't reach their ends.
There are 2 independent parts, one for each index of `groups`. The reference program is written for one: setup_inputs(seed, part) draws one part's arguments, and reference() takes and returns one part's arrays. A program takes and returns all parts, laid end to end along the dimension named above; an argument that names none is the same for every part. Nothing has to cross between parts.
Inputs may be any that keep to these rules, and one draw needn't show every extreme that they name: `slot_question`: every question is named by two or more answer choices; the 4 answer choices of one device name no question more than 2 times, and every device names some question exactly 2 times.
All inputs are finite; a program needn't handle non-finite values.
Results may differ from the reference program's by a relative error of at most 0.017.
Values may be sent and summed in bfloat16 or wider, within the bound.
A program may use at most 64 MiB of HBM per device.

```python
import math
import jax
import jax.numpy as jnp
from jax import lax

D = 4096
HEADS = 64
HD = 64
ENC = 256
ANS = 64
S_DEV = 4
QUESTIONS = 4
SLOTS = 16
ROWS = 1024
N_FSDP = 4


def draw_slot_question(key, part):
    pop_key, noise_key, rot_key, perm_key = jax.random.split(jax.random.fold_in(key, 11), 4)
    count = 2 * QUESTIONS
    candidate = jnp.arange(count, dtype=jnp.int32)
    cand_question = candidate // 2
    popularity = jax.random.randint(pop_key, (QUESTIONS,), 0, 5).astype(jnp.int32)
    noise = jax.random.randint(noise_key, (QUESTIONS, count), 0, 1024).astype(jnp.int32)
    rotation = jax.random.randint(rot_key, (), 0, QUESTIONS).astype(jnp.int32)
    devices = jnp.arange(QUESTIONS, dtype=jnp.int32)
    own = (devices + rotation) % QUESTIONS
    span = max(QUESTIONS - 1, 1)
    offset = (rotation + 1 + devices % span) % QUESTIONS
    second = (devices + offset) % QUESTIONS
    base = (popularity[cand_question][None, :] * 256 + noise) * count + candidate[None, :]
    scores = jnp.where(cand_question[None, :] == second[:, None], 16777216 + candidate[None, :], base)
    scores = jnp.where(cand_question[None, :] == own[:, None], 33554432 + candidate[None, :], scores).astype(jnp.int32)
    top_scores, top_index = lax.top_k(scores, S_DEV)
    picks = cand_question[top_index]
    shuffle = jax.random.randint(perm_key, (QUESTIONS, S_DEV), 0, 1048576).astype(jnp.int32) * S_DEV + jnp.arange(S_DEV, dtype=jnp.int32)[None, :]
    shuffled_scores, order = lax.top_k(shuffle, S_DEV)
    picks = jnp.take_along_axis(picks, order, axis=1)
    return picks.reshape(SLOTS).astype(jnp.int32)


def draw_enc_keys(key, part):
    base_key = jax.random.fold_in(jax.random.fold_in(key, 23), 0)
    shape = (QUESTIONS, ENC, HEADS * HD)
    values = jnp.clip(2.0 * jax.random.normal(base_key, shape, jnp.float32), -8.0, 8.0)
    return values.astype(jnp.bfloat16)


def plant(array, key, low, high):
    dims = array.shape
    place = [jax.random.randint(jax.random.fold_in(key, axis), (), 0, dims[axis]) for axis in range(len(dims))]
    array = array.at[tuple(place)].set(low)
    longest = dims.index(max(dims))
    place[longest] = (place[longest] + 1) % dims[longest]
    return array.at[tuple(place)].set(high)


def shard_levels(rng, dims, cuts, least, largest):
    gain, own = 1.0, jax.random.fold_in(rng, 6)
    for position, blocks in cuts:
        heights = jnp.exp(jax.random.uniform(jax.random.fold_in(own, position), (blocks,), jnp.float32, least / len(cuts), largest / len(cuts)))
        gain = gain * jnp.repeat(heights, dims[position] // blocks).reshape([-1 if axis == position else 1 for axis in range(len(dims))])
    return gain


def gaussian(rng, dims, spread, bound, cuts=(), held_as=jnp.bfloat16):
    result = spread * jax.random.normal(rng, dims, jnp.float32)
    if cuts:
        result = result * shard_levels(rng, dims, cuts, -0.22, 0.18)
    return jnp.clip(result, -bound, bound).astype(held_as)


def setup_inputs(seed: int = 0, part: int = 0) -> dict:
    key_list = jax.random.split(jax.random.key(seed), 9)
    part_splits = jax.random.split(jax.random.fold_in(key_list[8], part), 9)
    hidden = gaussian(part_splits[0], (ROWS, D), 1.0, 6.0, ((0, 4), (1, 4)))
    norm_gain = jnp.clip(1.0 + 0.15 * jax.random.normal(key_list[1], (D,), jnp.float32), 0.25, 1.75)
    query_weight = gaussian(key_list[2], (D, HEADS * HD), D ** -0.5, 0.09375, ((0, 4), (1, 4)))
    out_weight = gaussian(key_list[3], (HEADS * HD, D), (HEADS * HD) ** -0.5, 0.09375, ((0, 4), (1, 4)))
    enc_keys = draw_enc_keys(jax.random.fold_in(jax.random.fold_in(key_list[8], part), 71), part)
    enc_values = gaussian(part_splits[5], (QUESTIONS, ENC, HEADS * HD), 4.0, 24.0, ((0, 4), (2, 4)))
    slot_question = draw_slot_question(jax.random.fold_in(jax.random.fold_in(key_list[8], part), 71), part)
    answer_len = plant(jax.random.randint(part_splits[7], (SLOTS,), ANS // 4, ANS + 1), jax.random.fold_in(part_splits[7], 1), ANS // 4, ANS).astype(jnp.int32)
    return {"hidden": hidden, "norm_gain": norm_gain, "query_weight": query_weight, "out_weight": out_weight, "enc_keys": enc_keys, "enc_values": enc_values, "slot_question": slot_question, "answer_len": answer_len}


def reference(hidden, norm_gain, query_weight, out_weight, enc_keys, enc_values, slot_question, answer_len):
    widened = hidden.astype(jnp.float32)
    inverse = lax.rsqrt(lax.optimization_barrier(jnp.mean(widened * widened, axis=-1, keepdims=True)) + 1e-06)
    normed = (widened * inverse * norm_gain).astype(jnp.bfloat16)
    queries = jnp.dot(normed, query_weight, preferred_element_type=jnp.float32).astype(jnp.bfloat16)
    per_slot = queries.reshape(SLOTS, ANS, HEADS, HD)
    scale = 1.0 / math.sqrt(HD)

    def one_slot(operands):
        slot_queries, question = operands
        keys_block = lax.dynamic_index_in_dim(enc_keys, question, 0, keepdims=False).reshape(ENC, HEADS, HD)
        values_block = lax.dynamic_index_in_dim(enc_values, question, 0, keepdims=False).reshape(ENC, HEADS, HD)
        scores = jnp.einsum('ahd,khd->hak', slot_queries.astype(jnp.float32), keys_block.astype(jnp.float32)) * scale
        weights = jax.nn.softmax(scores, axis=-1).astype(jnp.bfloat16)
        context = jnp.einsum('hak,khd->ahd', weights.astype(jnp.float32), values_block.astype(jnp.float32))
        return context.astype(jnp.bfloat16).reshape(ANS, HEADS * HD)
    context = lax.map(one_slot, (per_slot, slot_question.astype(jnp.int32))).reshape(ROWS, HEADS * HD)
    group_width = HEADS * HD // N_FSDP

    def add_group(index, total):
        section = lax.dynamic_slice_in_dim(context, index * group_width, group_width, 1)
        panel = lax.dynamic_slice_in_dim(out_weight, index * group_width, group_width, 0)
        partial_sum = jnp.dot(section, panel, preferred_element_type=jnp.float32).astype(jnp.bfloat16)
        partial_sum = lax.optimization_barrier(partial_sum)
        return total + partial_sum.astype(jnp.float32)
    attended = lax.fori_loop(0, N_FSDP, add_group, jnp.zeros((ROWS, D), jnp.float32))
    positions = jnp.arange(ANS, dtype=jnp.int32)
    valid = (positions[None, :] < answer_len[:, None]).reshape(ROWS, 1)
    return jnp.where(valid, widened + attended, 0.0).astype(jnp.bfloat16)
```

```python
import functools
import math

import jax
import jax.numpy as jnp
from jax import lax
from jax.experimental import pallas as pl
from jax.experimental.pallas import tpu as pltpu
from jax.sharding import PartitionSpec as P

HD = 64
CAP = 2


epsilon = 1e-06


def flip(index, bits):
    result = index
    bit = 1
    while bit <= bits:
        if bits & bit:
            result = result + bit * (1 - 2 * ((index // bit) % 2))
        bit *= 2
    return result


def remote(src, dst, send_sem, recv_sem, axis, target):
    return pltpu.make_async_remote_copy(
        src_ref=src,
        dst_ref=dst,
        send_sem=send_sem,
        recv_sem=recv_sem,
        device_id={axis: target},
        device_id_type=pl.DeviceIdType.MESH,
    )


def block_kernel(
    C,
    F,
    answer_rows,
    hidden,
    gain,
    wq,
    wo,
    keys,
    values,
    questions,
    lengths,
    out,
    hrow,
    xs,
    xn,
    qs,
    qr,
    kb,
    vb,
    sq,
    sq_s,
    ctx,
    osend,
    orecv,
    asend,
    arecv,
    a_s,
    a_r,
    b_s,
    b_r,
    c_s,
    c_r,
    kv_s,
    kv_r,
    sq_ss,
    sq_r,
    d_s,
    d_r,
    e_s,
    e_r,
    g_s,
    g_r,
    h_s,
    h_r,
    local,
):
    c = lax.axis_index("choice")
    f = lax.axis_index("fsdp")
    rq = hidden.shape[0] // F
    df = hidden.shape[1]
    D = df * F
    kc = wq.shape[0]
    hc = wq.shape[1] // C
    rows = C * rq
    heads = hc // HD
    scale = 1.0 / math.sqrt(HD)

    choice_peers = [(lax.rem(c + t, C)) for t in range(1, C)]
    fsdp_peers = [flip(f, k) for k in range(1, F)]

    barrier = pltpu.get_barrier_semaphore()
    for p in choice_peers:
        pl.semaphore_signal(barrier, inc=1, device_id={"choice": p}, device_id_type=pl.DeviceIdType.MESH)
    for p in fsdp_peers:
        pl.semaphore_signal(barrier, inc=1, device_id={"fsdp": p}, device_id_type=pl.DeviceIdType.MESH)
    pl.semaphore_wait(barrier, C + F - 2)

    pending = []

    def send(*args):
        copy = remote(*args)
        copy.start()
        pending.append(copy)

    def arrived(dst, sem, axis):
        peer = choice_peers[0] if axis == "choice" else fsdp_peers[0]
        remote(dst, dst, sem, sem, axis, peer).wait_recv()

    def cols(index, width):
        return pl.ds(pl.multiple_of(index * width, width), width)

    def part(index):
        return pl.ds(pl.multiple_of(index * rq, rq), rq)

    for p in fsdp_peers:
        send(hidden.at[part(p)], hrow.at[:, cols(f, df)], a_s.at[p], a_r.at[f], "fsdp", p)
    hrow[:, cols(f, df)] = hidden[part(f), :]
    for p in fsdp_peers:
        arrived(hrow.at[:, cols(p, df)], a_r.at[p], "fsdp")

    total = jnp.zeros((rq, 1), jnp.float32)
    for i in range(F):
        x = hrow[:, i * df : (i + 1) * df].astype(jnp.float32)
        total = total + jnp.sum(x * x, axis=-1, keepdims=True)
    inverse = lax.rsqrt(total / D + epsilon)

    def norm_block(i):
        x = hrow[:, cols(i, kc)].astype(jnp.float32)
        return (x * inverse * gain[:, cols(i, kc)]).astype(jnp.bfloat16)

    for p in choice_peers:
        xs[p] = norm_block(p)
        send(xs.at[p], xn.at[f, c], b_s.at[p], b_r.at[c], "choice", p)
    xn[f, c] = norm_block(c)

    for p in fsdp_peers:
        send(xn.at[f, c], xn.at[f, c], c_s.at[p, c], c_r.at[f, c], "fsdp", p)
    for p in choice_peers:
        send(questions, sq.at[c], sq_ss.at[p], sq_r.at[c], "choice", p)
    for p in choice_peers:
        arrived(xn.at[f, p], b_r.at[p], "choice")
        for o in fsdp_peers:
            send(xn.at[f, p], xn.at[f, p], c_s.at[o, p], c_r.at[f, p], "fsdp", o)

    for p in choice_peers:
        send(keys.at[:, cols(p, hc)], kb.at[c], kv_s.at[0, p], kv_r.at[0, c], "choice", p)
        send(values.at[:, cols(p, hc)], vb.at[c], kv_s.at[1, p], kv_r.at[1, c], "choice", p)
    kb[c] = keys[:, cols(c, hc)]
    vb[c] = values[:, cols(c, hc)]
    sq[c] = questions[...]

    head_of_lane = lax.broadcasted_iota(jnp.int32, (1, hc), 1) // HD

    def project(k):
        j = flip(f, k)
        if k > 0:
            for i in range(C):
                arrived(xn.at[j, i], c_r.at[j, i], "fsdp")
        for t in range(1, C + 1):
            p = lax.rem(c + t, C)
            acc = jnp.dot(
                xn[j].reshape(rows, kc), wq[:, cols(p, hc)], preferred_element_type=jnp.float32
            ).astype(jnp.bfloat16)
            if t < C:
                qs[j, p] = acc
                send(qs.at[j, p], qr.at[j, c], d_s.at[j, p], d_r.at[j, c], "choice", p)
            else:
                qr[j, c] = acc

    def attend(k):
        j = flip(f, k)
        if k == 0:
            for p in choice_peers:
                arrived(sq.at[p], sq_r.at[p], "choice")
            copy = pltpu.make_async_copy(sq, sq_s, local)
            copy.start()
            copy.wait()
        for p in choice_peers:
            arrived(qr.at[j, p], d_r.at[j, p], "choice")
        if k == 0:
            for p in choice_peers:
                arrived(kb.at[p], kv_r.at[0, p], "choice")
                arrived(vb.at[p], kv_r.at[1, p], "choice")

        def one(step, carry):
            i = step // (rq // answer_rows)
            inner = step % (rq // answer_rows)
            q = sq_s[i, 0, j * (rq // answer_rows) + inner]
            here = pl.ds(pl.multiple_of(step * answer_rows, answer_rows), answer_rows)
            query = qr[j, 0, here, :].astype(jnp.float32)
            for s in range(1, C):
                query = query + qr[j, s, here, :].astype(jnp.float32)
            query = query.astype(jnp.bfloat16)
            zero = jnp.zeros_like(query)
            stacked = jnp.concatenate(
                [jnp.where(head_of_lane == h, query, zero) for h in range(heads)], axis=0
            )
            scores = lax.dot_general(
                stacked, kb[q], (((1,), (1,)), ((), ())), preferred_element_type=jnp.float32
            ) * scale
            top = jnp.max(scores, axis=-1, keepdims=True)
            e = jnp.exp(scores - top)
            weights = (e * (1.0 / jnp.sum(e, axis=-1, keepdims=True))).astype(jnp.bfloat16)
            mixed = jnp.dot(weights, vb[q], preferred_element_type=jnp.float32)
            found = mixed[:answer_rows]
            for h in range(1, heads):
                found = jnp.where(head_of_lane == h, mixed[h * answer_rows : (h + 1) * answer_rows], found)
            ctx[j, c, here, :] = found.astype(jnp.bfloat16)
            return carry

        lax.fori_loop(0, rows // answer_rows, one, 0)
        for p in choice_peers:
            send(ctx.at[j, c], ctx.at[j, c], e_s.at[j, p], e_r.at[j, c], "choice", p)

    def mix(k):
        j = flip(f, k)
        for p in choice_peers:
            arrived(ctx.at[j, p], e_r.at[j, p], "choice")
        tile = hc
        for t in range(kc // tile):
            acc = jnp.dot(ctx[j, 0], wo[0:hc, t * tile : (t + 1) * tile], preferred_element_type=jnp.float32)
            for s in range(1, C):
                acc = acc + jnp.dot(
                    ctx[j, s],
                    wo[s * hc : (s + 1) * hc, t * tile : (t + 1) * tile],
                    preferred_element_type=jnp.float32,
                )
            acc = acc.astype(jnp.bfloat16)
            if k > 0:
                osend[j, :, t * tile : (t + 1) * tile] = acc
            else:
                orecv[j, :, t * tile : (t + 1) * tile] = acc
        if k > 0:
            send(osend.at[j], orecv.at[f], g_s.at[j], g_r.at[f], "fsdp", j)

    for k in range(F + 2):
        if k < F:
            project(k)
        if 1 <= k <= F:
            attend(k - 1)
        if k >= 2:
            mix(k - 2)

    for p in fsdp_peers:
        arrived(orecv.at[p], g_r.at[p], "fsdp")

    def gathered(i):
        here = pl.ds(pl.multiple_of(i * rq, rq), rq)
        acc = orecv[0, here, :].astype(jnp.float32)
        for s in range(1, F):
            acc = acc + orecv[s, here, :].astype(jnp.float32)
        return acc.astype(jnp.bfloat16)

    for p in choice_peers:
        asend[p] = gathered(p)
        send(asend.at[p], arecv.at[c], h_s.at[p], h_r.at[c], "choice", p)
    arecv[c] = gathered(c)

    position = f * rq + lax.broadcasted_iota(jnp.int32, (rq, 1), 0)
    slot = position // answer_rows
    length = jnp.zeros((rq, 1), jnp.int32)
    for s in range(lengths.shape[0]):
        length = jnp.where(slot == s, lengths[s], length)
    valid = position % answer_rows < length

    def finish(i):
        x = hrow[:, cols(i, kc)].astype(jnp.float32) + arecv[i].astype(jnp.float32)
        out[:, cols(i, kc)] = jnp.where(valid, x, 0.0).astype(jnp.bfloat16)

    finish(c)
    for p in choice_peers:
        arrived(arecv.at[p], h_r.at[p], "choice")
        finish(p)
    for copy in pending:
        copy.wait_send()


def in_one_kernel(
    C, F, hidden, norm_gain, query_weight, out_weight, enc_keys, enc_values, slot_question, answer_len
):
    count = hidden.shape[0]
    rq = count // F
    df = hidden.shape[1]
    D = df * F
    kc, width = query_weight.shape
    hc = width // C
    rows = C * rq
    enc = enc_keys.shape[1]
    slots = slot_question.shape[0]
    questions = jnp.pad(slot_question[None, :], ((0, 7), (0, 128 - slots)))
    bf = jnp.bfloat16
    vmem = pl.BlockSpec(memory_space=pltpu.VMEM)
    dma = pltpu.SemaphoreType.DMA
    return pl.pallas_call(
        functools.partial(block_kernel, C, F, count // slots),
        out_shape=jax.ShapeDtypeStruct((rq, D), bf),
        in_specs=[vmem] * 7 + [pl.BlockSpec(memory_space=pltpu.SMEM)],
        out_specs=vmem,
        scratch_shapes=[
            pltpu.VMEM((rq, D), bf),
            pltpu.VMEM((C, rq, kc), bf),
            pltpu.VMEM((F, C, rq, kc), bf),
            pltpu.VMEM((F, C, rows, hc), bf),
            pltpu.VMEM((F, C, rows, hc), bf),
            pltpu.VMEM((C, enc, hc), bf),
            pltpu.VMEM((C, enc, hc), bf),
            pltpu.VMEM((C, 8, 128), jnp.int32),
            pltpu.SMEM((C, 8, 128), jnp.int32),
            pltpu.VMEM((F, C, rows, hc), bf),
            pltpu.VMEM((F, rows, kc), bf),
            pltpu.VMEM((F, rows, kc), bf),
            pltpu.VMEM((C, rq, kc), bf),
            pltpu.VMEM((C, rq, kc), bf),
            dma((F,)),
            dma((F,)),
            dma((C,)),
            dma((C,)),
            dma((F, C)),
            dma((F, C)),
            dma((2, C)),
            dma((2, C)),
            dma((C,)),
            dma((C,)),
            dma((F, C)),
            dma((F, C)),
            dma((F, C)),
            dma((F, C)),
            dma((F,)),
            dma((F,)),
            dma((C,)),
            dma((C,)),
            dma,
        ],
        compiler_params=pltpu.CompilerParams(
            collective_id=0, has_side_effects=True, vmem_limit_bytes=50 * 1024 * 1024
        ),
        cost_estimate=pl.CostEstimate(
            flops=4 * F * rows * kc * width, bytes_accessed=8 * kc * width, transcendentals=F * rows * enc * (hc // HD)
        ),
    )(
        hidden,
        norm_gain.reshape(1, D),
        query_weight,
        out_weight,
        enc_keys[0],
        enc_values[0],
        questions,
        answer_len,
    )


def attend_rows(query_rows, keys_block, values_block):
    count = query_rows.shape[0]
    width = query_rows.shape[1]
    heads_here = width // HD
    scale = 1.0 / math.sqrt(HD)
    query_view = query_rows.reshape(count, heads_here, HD)
    key_view = keys_block.reshape(keys_block.shape[0], heads_here, HD)
    value_view = values_block.reshape(values_block.shape[0], heads_here, HD)
    scores = (
        jnp.einsum("ahd,khd->hak", query_view, key_view, preferred_element_type=jnp.float32) * scale
    )
    weights = jax.nn.softmax(scores, axis=-1).astype(jnp.bfloat16)
    context = jnp.einsum("hak,khd->ahd", weights, value_view, preferred_element_type=jnp.float32)
    return context.astype(jnp.bfloat16).reshape(count, width)


def picked(choose, blocks):
    return jnp.einsum(
        "bs,sax->bax", choose.astype(jnp.bfloat16), blocks, preferred_element_type=jnp.float32
    ).astype(jnp.bfloat16)


def on_device(
    hidden, norm_gain, query_weight, out_weight, enc_keys, enc_values, slot_question, answer_len
):
    whole = lax.all_gather(hidden, "fsdp", axis=1, tiled=True)
    widened = whole.astype(jnp.float32)
    total_rows = widened.shape[0]
    slots_here = slot_question.shape[0]
    answer_rows = total_rows // slots_here
    inverse = lax.rsqrt(jnp.mean(widened * widened, axis=-1, keepdims=True) + epsilon)
    normed = (widened * inverse * norm_gain).astype(jnp.bfloat16)
    columns = query_weight.shape[1]
    section = normed
    queries = jnp.dot(
        section,
        lax.all_gather(query_weight, "choice", axis=0, tiled=True),
        preferred_element_type=jnp.float32,
    ).astype(jnp.bfloat16)
    per_slot = queries.reshape(slots_here, answer_rows, columns)
    owners = lax.axis_size("choice")
    buffers = owners * CAP
    slot_ids = jnp.arange(slots_here, dtype=jnp.int32)
    earlier = slot_ids[:, None] > slot_ids[None, :]
    same_question = slot_question[:, None] == slot_question[None, :]
    rank = jnp.sum(jnp.where(same_question & earlier, 1, 0), axis=1).astype(jnp.int32)
    target = slot_question * CAP + rank
    placed = jnp.arange(buffers, dtype=jnp.int32)[:, None] == target[None, :]
    outgoing = picked(placed, per_slot)
    outgoing = outgoing.reshape(owners, CAP, answer_rows, columns)
    local_keys = enc_keys[0]
    local_values = enc_values[0]

    def answer_source(block):
        flat_rows = block.reshape(-1, columns)
        return attend_rows(flat_rows, local_keys, local_values).reshape(block.shape)

    answered = lax.map(
        answer_source, lax.all_to_all(outgoing, "choice", split_axis=0, concat_axis=0, tiled=True)
    )
    returned = lax.all_to_all(answered, "choice", split_axis=0, concat_axis=0, tiled=True)
    context = picked(placed.T, returned.reshape(buffers, answer_rows, columns))
    context_rows = context.reshape(total_rows, columns)
    out_full = lax.all_gather(out_weight, "choice", axis=1, tiled=True)
    share = total_rows // lax.axis_size("fsdp")
    section = context_rows
    mixed = lax.psum_scatter(
        jnp.dot(section, out_full, preferred_element_type=jnp.float32).astype(jnp.bfloat16),
        "fsdp",
        scatter_dimension=0,
        tiled=True,
    ).astype(jnp.float32)
    offset = lax.axis_index("fsdp") * share
    residual = lax.dynamic_slice_in_dim(widened, offset, share, 0)
    positions = offset + jnp.arange(share, dtype=jnp.int32)
    slot_index = positions // answer_rows
    matching = slot_index[:, None] == jnp.arange(slots_here, dtype=jnp.int32)[None, :]
    lengths = jnp.sum(jnp.where(matching, answer_len[None, :], 0), axis=1)
    valid = positions % answer_rows < lengths
    return jnp.where(valid[:, None], residual + mixed, 0.0).astype(jnp.bfloat16)


def solution(mesh):
    in_specs = (
        P(("groups", "choice"), "fsdp"),
        P(),
        P("choice", "fsdp"),
        P("fsdp", "choice"),
        P(("groups", "choice"), None, "fsdp"),
        P(("groups", "choice"), None, "fsdp"),
        P(("groups", "choice")),
        P(("groups", "choice")),
    )
    out_specs = P(("groups", "choice", "fsdp"), None)
    C = mesh.shape["choice"]
    F = mesh.shape["fsdp"]

    def body(*args):
        hidden, query_weight, slot_question = args[0], args[2], args[6]
        count = hidden.shape[0]
        answer_rows = count // slot_question.shape[0]
        fits = (
            F & (F - 1) == 0
            and count % F == 0
            and (count // F) % answer_rows == 0
            and query_weight.shape[1] % (C * 128) == 0
            and query_weight.shape[0] % (query_weight.shape[1] // C) == 0
            and F > 1
            and C > 1
        )
        return in_one_kernel(C, F, *args) if fits else on_device(*args)

    return jax.shard_map(
        body, mesh=mesh, in_specs=in_specs, out_specs=out_specs, check_vma=False
    )
```

```python
import functools
import math

import jax
import jax.numpy as jnp
from jax import lax
from jax.experimental import pallas as pl
from jax.experimental.pallas import tpu as pltpu
from jax.sharding import PartitionSpec as P

HD = 64
CAP = 2


epsilon = 1e-06


def flip(index, bits):
    result = index
    bit = 1
    while bit <= bits:
        if bits & bit:
            result = result + bit * (1 - 2 * ((index // bit) % 2))
        bit *= 2
    return result


def remote(src, dst, send_sem, recv_sem, axis, target):
    return pltpu.make_async_remote_copy(
        src_ref=src,
        dst_ref=dst,
        send_sem=send_sem,
        recv_sem=recv_sem,
        device_id={axis: target},
        device_id_type=pl.DeviceIdType.MESH,
    )


def block_kernel(
    C,
    F,
    answer_rows,
    hidden,
    gain,
    wq_hbm,
    wo_hbm,
    keys,
    values,
    questions,
    lengths,
    out,
    hrow,
    wq,
    wo,
    xs,
    xn,
    qs,
    qr,
    kb,
    vb,
    sq,
    sq_s,
    ctx,
    osend,
    orecv,
    asend,
    arecv,
    a_s,
    a_r,
    b_s,
    b_r,
    c_s,
    c_r,
    kv_s,
    kv_r,
    sq_ss,
    sq_r,
    d_s,
    d_r,
    e_s,
    e_r,
    g_s,
    g_r,
    h_s,
    h_r,
    local,
):
    c = lax.axis_index("choice")
    f = lax.axis_index("fsdp")
    rq = hidden.shape[0] // F
    df = hidden.shape[1]
    D = df * F
    kc = wq.shape[0]
    hc = wq.shape[1] // C
    rows = C * rq
    heads = hc // HD
    scale = 1.0 / math.sqrt(HD)

    choice_peers = [(lax.rem(c + t, C)) for t in range(1, C)]
    fsdp_peers = [flip(f, k) for k in range(1, F)]

    barrier = pltpu.get_barrier_semaphore()
    for p in choice_peers:
        pl.semaphore_signal(barrier, inc=1, device_id={"choice": p}, device_id_type=pl.DeviceIdType.MESH)
    for p in fsdp_peers:
        pl.semaphore_signal(barrier, inc=1, device_id={"fsdp": p}, device_id_type=pl.DeviceIdType.MESH)
    pl.semaphore_wait(barrier, C + F - 2)

    pending = []

    def send(*args):
        copy = remote(*args)
        copy.start()
        pending.append(copy)

    def arrived(dst, sem, axis):
        peer = choice_peers[0] if axis == "choice" else fsdp_peers[0]
        remote(dst, dst, sem, sem, axis, peer).wait_recv()

    def cols(index, width):
        return pl.ds(pl.multiple_of(index * width, width), width)

    def part(index):
        return pl.ds(pl.multiple_of(index * rq, rq), rq)

    for p in fsdp_peers:
        send(hidden.at[part(p)], hrow.at[:, cols(f, df)], a_s.at[p], a_r.at[f], "fsdp", p)
    def bring(src, dst, i):
        copy = pltpu.make_async_copy(src, dst, local.at[i])
        copy.start()
        return copy

    own_rows = bring(hidden.at[part(f)], hrow.at[:, cols(f, df)], 0)
    own_keys = bring(keys.at[:, cols(c, hc)], kb.at[c], 1)
    query_copy = bring(wq_hbm, wq, 2)
    own_values = bring(values.at[:, cols(c, hc)], vb.at[c], 3)
    out_copy = bring(wo_hbm, wo, 4)
    for p in choice_peers:
        send(keys.at[:, cols(p, hc)], kb.at[c], kv_s.at[0, p], kv_r.at[0, c], "choice", p)
    own_rows.wait()
    for p in fsdp_peers:
        arrived(hrow.at[:, cols(p, df)], a_r.at[p], "fsdp")

    total = jnp.zeros((rq, 1), jnp.float32)
    for i in range(F):
        x = hrow[:, i * df : (i + 1) * df].astype(jnp.float32)
        total = total + jnp.sum(x * x, axis=-1, keepdims=True)
    inverse = lax.rsqrt(total / D + epsilon)

    def norm_block(i):
        x = hrow[:, cols(i, kc)].astype(jnp.float32)
        return (x * inverse * gain[:, cols(i, kc)]).astype(jnp.bfloat16)

    for p in choice_peers:
        xs[p] = norm_block(p)
        send(xs.at[p], xn.at[f, c], b_s.at[p], b_r.at[c], "choice", p)
    xn[f, c] = norm_block(c)

    for p in fsdp_peers:
        send(xn.at[f, c], xn.at[f, c], c_s.at[p, c], c_r.at[f, c], "fsdp", p)
    for p in choice_peers:
        send(questions, sq.at[c], sq_ss.at[p], sq_r.at[c], "choice", p)
    for p in choice_peers:
        arrived(xn.at[f, p], b_r.at[p], "choice")
        for o in fsdp_peers:
            send(xn.at[f, p], xn.at[f, p], c_s.at[o, p], c_r.at[f, p], "fsdp", o)

    for p in choice_peers:
        send(values.at[:, cols(p, hc)], vb.at[c], kv_s.at[1, p], kv_r.at[1, c], "choice", p)
    sq[c] = questions[...]

    head_of_lane = lax.broadcasted_iota(jnp.int32, (1, hc), 1) // HD

    def project(k):
        j = flip(f, k)
        if k == 0:
            query_copy.wait()
        else:
            for i in range(C):
                arrived(xn.at[j, i], c_r.at[j, i], "fsdp")
        for t in range(1, C + 1):
            p = lax.rem(c + t, C)
            acc = jnp.dot(
                xn[j].reshape(rows, kc), wq[:, cols(p, hc)], preferred_element_type=jnp.float32
            ).astype(jnp.bfloat16)
            if t < C:
                qs[j, p] = acc
                send(qs.at[j, p], qr.at[j, c], d_s.at[j, p], d_r.at[j, c], "choice", p)
            else:
                qr[j, c] = acc

    def attend(k):
        j = flip(f, k)
        if k == 0:
            for p in choice_peers:
                arrived(sq.at[p], sq_r.at[p], "choice")
            copy = pltpu.make_async_copy(sq, sq_s, local.at[5])
            copy.start()
            copy.wait()
        for p in choice_peers:
            arrived(qr.at[j, p], d_r.at[j, p], "choice")
        if k == 0:
            own_keys.wait()
            own_values.wait()
            for p in choice_peers:
                arrived(kb.at[p], kv_r.at[0, p], "choice")
                arrived(vb.at[p], kv_r.at[1, p], "choice")

        def one(step, carry):
            i = step // (rq // answer_rows)
            inner = step % (rq // answer_rows)
            q = sq_s[i, 0, j * (rq // answer_rows) + inner]
            here = pl.ds(pl.multiple_of(step * answer_rows, answer_rows), answer_rows)
            query = qr[j, 0, here, :].astype(jnp.float32)
            for s in range(1, C):
                query = query + qr[j, s, here, :].astype(jnp.float32)
            query = query.astype(jnp.bfloat16)
            zero = jnp.zeros_like(query)
            stacked = jnp.concatenate(
                [jnp.where(head_of_lane == h, query, zero) for h in range(heads)], axis=0
            )
            scores = lax.dot_general(
                stacked, kb[q], (((1,), (1,)), ((), ())), preferred_element_type=jnp.float32
            ) * scale
            top = jnp.max(scores, axis=-1, keepdims=True)
            e = jnp.exp(scores - top)
            weights = (e * (1.0 / jnp.sum(e, axis=-1, keepdims=True))).astype(jnp.bfloat16)
            mixed = jnp.dot(weights, vb[q], preferred_element_type=jnp.float32)
            found = mixed[:answer_rows]
            for h in range(1, heads):
                found = jnp.where(head_of_lane == h, mixed[h * answer_rows : (h + 1) * answer_rows], found)
            ctx[j, c, here, :] = found.astype(jnp.bfloat16)
            return carry

        lax.fori_loop(0, rows // answer_rows, one, 0)
        pass_on(j, c, 1)
        pass_on(j, c, -1)

    def has(step):
        return c < C - 1 if step > 0 else c > 0

    def hop(j, s, step):
        return remote(
            ctx.at[j, s], ctx.at[j, s], e_s.at[(step + 1) // 2, j, s], e_r.at[j, s], "choice", lax.rem(c + step + C, C)
        )

    def pass_on(j, s, step):
        @pl.when(has(step))
        def _():
            hop(j, s, step).start()

    def relay(k):
        j = flip(f, k)
        for t in range(1, C):
            for step in (1, -1):
                s = c - t * step

                @pl.when((s >= 0) & (s < C))
                def _():
                    arrived(ctx.at[j, s], e_r.at[j, s], "choice")
                    pass_on(j, s, step)

    def settle(k):
        j = flip(f, k)
        for t in range(C):
            for step in (1, -1):
                s = c - t * step

                @pl.when((s >= 0) & (s < C) & has(step))
                def _():
                    hop(j, s, step).wait_send()

    def mix(k):
        j = flip(f, k)
        relay(k)
        if k == 0:
            out_copy.wait()
        tile = hc
        for t in range(kc // tile):
            acc = jnp.dot(ctx[j, 0], wo[0:hc, t * tile : (t + 1) * tile], preferred_element_type=jnp.float32)
            for s in range(1, C):
                acc = acc + jnp.dot(
                    ctx[j, s],
                    wo[s * hc : (s + 1) * hc, t * tile : (t + 1) * tile],
                    preferred_element_type=jnp.float32,
                )
            acc = acc.astype(jnp.bfloat16)
            if k > 0:
                osend[j, :, t * tile : (t + 1) * tile] = acc
            else:
                orecv[j, :, t * tile : (t + 1) * tile] = acc
        if k > 0:
            for i in choice_peers + [c]:
                send(osend.at[j, part(i)], orecv.at[f, part(i)], g_s.at[j, i], g_r.at[f, i], "fsdp", j)

    order = [0] + list(range(2, F)) + [1]
    for k in range(F + 2):
        if k < F:
            project(order[k])
        if 1 <= k <= F:
            attend(order[k - 1])
        if k >= 2:
            mix(order[k - 2])

    def gathered(i):
        here = part(i)
        for p in fsdp_peers:
            arrived(orecv.at[p, here], g_r.at[p, i], "fsdp")
        acc = orecv[0, here, :].astype(jnp.float32)
        for s in range(1, F):
            acc = acc + orecv[s, here, :].astype(jnp.float32)
        return acc.astype(jnp.bfloat16)

    for p in choice_peers:
        asend[p] = gathered(p)
        send(asend.at[p], arecv.at[c], h_s.at[p], h_r.at[c], "choice", p)
    arecv[c] = gathered(c)

    position = f * rq + lax.broadcasted_iota(jnp.int32, (rq, 1), 0)
    slot = position // answer_rows
    length = jnp.zeros((rq, 1), jnp.int32)
    for s in range(lengths.shape[0]):
        length = jnp.where(slot == s, lengths[s], length)
    valid = position % answer_rows < length

    def finish(i):
        x = hrow[:, cols(i, kc)].astype(jnp.float32) + arecv[i].astype(jnp.float32)
        out[:, cols(i, kc)] = jnp.where(valid, x, 0.0).astype(jnp.bfloat16)

    finish(c)
    for p in choice_peers:
        arrived(arecv.at[p], h_r.at[p], "choice")
        finish(p)
    for copy in pending:
        copy.wait_send()
    for k in range(F):
        settle(k)


def in_one_kernel(
    C, F, hidden, norm_gain, query_weight, out_weight, enc_keys, enc_values, slot_question, answer_len
):
    count = hidden.shape[0]
    rq = count // F
    df = hidden.shape[1]
    D = df * F
    kc, width = query_weight.shape
    hc = width // C
    rows = C * rq
    enc = enc_keys.shape[1]
    slots = slot_question.shape[0]
    questions = jnp.pad(slot_question[None, :], ((0, 7), (0, 128 - slots)))
    bf = jnp.bfloat16
    vmem = pl.BlockSpec(memory_space=pltpu.VMEM)
    hbm = pl.BlockSpec(memory_space=pl.ANY)
    dma = pltpu.SemaphoreType.DMA
    return pl.pallas_call(
        functools.partial(block_kernel, C, F, count // slots),
        out_shape=jax.ShapeDtypeStruct((rq, D), bf),
        in_specs=[hbm, vmem, hbm, hbm, hbm, hbm, vmem] + [pl.BlockSpec(memory_space=pltpu.SMEM)],
        out_specs=vmem,
        scratch_shapes=[
            pltpu.VMEM((rq, D), bf),
            pltpu.VMEM((kc, width), bf),
            pltpu.VMEM((width, kc), bf),
            pltpu.VMEM((C, rq, kc), bf),
            pltpu.VMEM((F, C, rq, kc), bf),
            pltpu.VMEM((F, C, rows, hc), bf),
            pltpu.VMEM((F, C, rows, hc), bf),
            pltpu.VMEM((C, enc, hc), bf),
            pltpu.VMEM((C, enc, hc), bf),
            pltpu.VMEM((C, 8, 128), jnp.int32),
            pltpu.SMEM((C, 8, 128), jnp.int32),
            pltpu.VMEM((F, C, rows, hc), bf),
            pltpu.VMEM((F, rows, kc), bf),
            pltpu.VMEM((F, rows, kc), bf),
            pltpu.VMEM((C, rq, kc), bf),
            pltpu.VMEM((C, rq, kc), bf),
            dma((F,)),
            dma((F,)),
            dma((C,)),
            dma((C,)),
            dma((F, C)),
            dma((F, C)),
            dma((2, C)),
            dma((2, C)),
            dma((C,)),
            dma((C,)),
            dma((F, C)),
            dma((F, C)),
            dma((2, F, C)),
            dma((F, C)),
            dma((F, C)),
            dma((F, C)),
            dma((C,)),
            dma((C,)),
            dma((6,)),
        ],
        compiler_params=pltpu.CompilerParams(
            collective_id=0, has_side_effects=True, vmem_limit_bytes=50 * 1024 * 1024
        ),
        cost_estimate=pl.CostEstimate(
            flops=4 * F * rows * kc * width, bytes_accessed=8 * kc * width, transcendentals=F * rows * enc * (hc // HD)
        ),
    )(
        hidden,
        norm_gain.reshape(1, D),
        query_weight,
        out_weight,
        enc_keys[0],
        enc_values[0],
        questions,
        answer_len,
    )


def attend_rows(query_rows, keys_block, values_block):
    count = query_rows.shape[0]
    width = query_rows.shape[1]
    heads_here = width // HD
    scale = 1.0 / math.sqrt(HD)
    query_view = query_rows.reshape(count, heads_here, HD)
    key_view = keys_block.reshape(keys_block.shape[0], heads_here, HD)
    value_view = values_block.reshape(values_block.shape[0], heads_here, HD)
    scores = (
        jnp.einsum("ahd,khd->hak", query_view, key_view, preferred_element_type=jnp.float32) * scale
    )
    weights = jax.nn.softmax(scores, axis=-1).astype(jnp.bfloat16)
    context = jnp.einsum("hak,khd->ahd", weights, value_view, preferred_element_type=jnp.float32)
    return context.astype(jnp.bfloat16).reshape(count, width)


def picked(choose, blocks):
    return jnp.einsum(
        "bs,sax->bax", choose.astype(jnp.bfloat16), blocks, preferred_element_type=jnp.float32
    ).astype(jnp.bfloat16)


def on_device(
    hidden, norm_gain, query_weight, out_weight, enc_keys, enc_values, slot_question, answer_len
):
    whole = lax.all_gather(hidden, "fsdp", axis=1, tiled=True)
    widened = whole.astype(jnp.float32)
    total_rows = widened.shape[0]
    slots_here = slot_question.shape[0]
    answer_rows = total_rows // slots_here
    inverse = lax.rsqrt(jnp.mean(widened * widened, axis=-1, keepdims=True) + epsilon)
    normed = (widened * inverse * norm_gain).astype(jnp.bfloat16)
    columns = query_weight.shape[1]
    section = normed
    queries = jnp.dot(
        section,
        lax.all_gather(query_weight, "choice", axis=0, tiled=True),
        preferred_element_type=jnp.float32,
    ).astype(jnp.bfloat16)
    per_slot = queries.reshape(slots_here, answer_rows, columns)
    owners = lax.axis_size("choice")
    buffers = owners * CAP
    slot_ids = jnp.arange(slots_here, dtype=jnp.int32)
    earlier = slot_ids[:, None] > slot_ids[None, :]
    same_question = slot_question[:, None] == slot_question[None, :]
    rank = jnp.sum(jnp.where(same_question & earlier, 1, 0), axis=1).astype(jnp.int32)
    target = slot_question * CAP + rank
    placed = jnp.arange(buffers, dtype=jnp.int32)[:, None] == target[None, :]
    outgoing = picked(placed, per_slot)
    outgoing = outgoing.reshape(owners, CAP, answer_rows, columns)
    local_keys = enc_keys[0]
    local_values = enc_values[0]

    def answer_source(block):
        flat_rows = block.reshape(-1, columns)
        return attend_rows(flat_rows, local_keys, local_values).reshape(block.shape)

    answered = lax.map(
        answer_source, lax.all_to_all(outgoing, "choice", split_axis=0, concat_axis=0, tiled=True)
    )
    returned = lax.all_to_all(answered, "choice", split_axis=0, concat_axis=0, tiled=True)
    context = picked(placed.T, returned.reshape(buffers, answer_rows, columns))
    context_rows = context.reshape(total_rows, columns)
    out_full = lax.all_gather(out_weight, "choice", axis=1, tiled=True)
    share = total_rows // lax.axis_size("fsdp")
    section = context_rows
    mixed = lax.psum_scatter(
        jnp.dot(section, out_full, preferred_element_type=jnp.float32).astype(jnp.bfloat16),
        "fsdp",
        scatter_dimension=0,
        tiled=True,
    ).astype(jnp.float32)
    offset = lax.axis_index("fsdp") * share
    residual = lax.dynamic_slice_in_dim(widened, offset, share, 0)
    positions = offset + jnp.arange(share, dtype=jnp.int32)
    slot_index = positions // answer_rows
    matching = slot_index[:, None] == jnp.arange(slots_here, dtype=jnp.int32)[None, :]
    lengths = jnp.sum(jnp.where(matching, answer_len[None, :], 0), axis=1)
    valid = positions % answer_rows < lengths
    return jnp.where(valid[:, None], residual + mixed, 0.0).astype(jnp.bfloat16)


def solution(mesh):
    in_specs = (
        P(("groups", "choice"), "fsdp"),
        P(),
        P("choice", "fsdp"),
        P("fsdp", "choice"),
        P(("groups", "choice"), None, "fsdp"),
        P(("groups", "choice"), None, "fsdp"),
        P(("groups", "choice")),
        P(("groups", "choice")),
    )
    out_specs = P(("groups", "choice", "fsdp"), None)
    C = mesh.shape["choice"]
    F = mesh.shape["fsdp"]

    def body(*args):
        hidden, query_weight, slot_question = args[0], args[2], args[6]
        count = hidden.shape[0]
        answer_rows = count // slot_question.shape[0]
        fits = (
            F & (F - 1) == 0
            and count % F == 0
            and (count // F) % answer_rows == 0
            and query_weight.shape[1] % (C * 128) == 0
            and query_weight.shape[0] % (query_weight.shape[1] // C) == 0
            and F > 1
            and C > 1
        )
        return in_one_kernel(C, F, *args) if fits else on_device(*args)

    return jax.shard_map(
        body, mesh=mesh, in_specs=in_specs, out_specs=out_specs, check_vma=False
    )
```
